256 devices in a mesh: seq: 64 (over z_hi, y, x), head: 4 (over z_lo, core).
Axes of the slice: x: 4, y: 4, z: 8 (z_hi: 4, z_lo: 2; z = z_hi * 2 + z_lo), core: 2. Of those that a mesh axis runs over, the one named last changes fastest.
Arguments:
- queries: bfloat16 [3, 16384, 2048], P(None, 'seq', 'head'), may hold values from -24 to 24
- key_vectors: bfloat16 [4, 16384, 2048], P(None, 'seq', 'head'), may hold values from -24 to 24
- values: bfloat16 [4, 16384, 2048], P(None, 'seq', 'head'), may hold values from -6 to 6
- learn_rates: float32 [3, 16384, 4], P(None, 'seq', 'head'), may hold values from 0.001 to 0.01
- norm_gain: float32 [2048], P('head'), may hold values from 0.1 to 1.9
- out_weight: bfloat16 [2048, 2048], P('head'), may hold values from -0.125 to 0.125
- incoming: float32 [64, 4, 3, 512, 512], P('seq', 'head'), may hold values from -0.25 to 0.25
Outputs:
- mixed_out: bfloat16 [3, 16384, 2048], P(None, 'seq', 'head')
- outgoing: float32 [64, 4, 3, 512, 512], P('seq', 'head')
The draws below stay inside these ranges and needn't reach their ends.
All inputs are finite; a program needn't handle non-finite values.
Results may differ from the reference program's by a relative error of at most 0.013.
The reference program's roundings to bfloat16 on the way count: a program that leaves them out, or rounds other values in their place, can miss the bound.
Values may be sent and summed in bfloat16 or wider, within the bound.
No kernel may reach another device: no remote copies, remote signals or barrier semaphores. Data moves between devices by JAX's collectives and lax.ppermute only.
A program may use at most 64 MiB of HBM per device.

```python
import math
import jax
import jax.numpy as jnp
from jax import lax

HEADS = 4
HD = 512
GROUP = 256
TICKS = 3
WIDTH = 2048
SEQ_TOK = 16384
N_SEQ = 64


def paired_draw(key):
    key_raw = jax.random.normal(jax.random.fold_in(key, 101), (TICKS + 1, SEQ_TOK, WIDTH), jnp.float32)
    query_raw = jax.random.normal(jax.random.fold_in(key, 202), (TICKS, SEQ_TOK, WIDTH), jnp.float32)
    return (jnp.clip(key_raw, -24.0, 24.0), jnp.clip(query_raw, -24.0, 24.0))


def draw_queries(key, part):
    return paired_draw(key)[1].astype(jnp.bfloat16)


def draw_key_vectors(key, part):
    return paired_draw(key)[0].astype(jnp.bfloat16)


def levels(rng, shape, cuts, low, largest):
    def one(axis_at, shards_of):
        draws = jax.random.uniform(jax.random.fold_in(jax.random.fold_in(rng, 6), axis_at), (shards_of,), jnp.float32, low / len(cuts), largest / len(cuts))
        return jnp.repeat(jnp.exp(draws), shape[axis_at] // shards_of).reshape((-1,) + (1,) * (len(shape) - axis_at - 1))

    gain = one(*cuts[0])
    for cut in cuts[1:]:
        gain = gain * one(*cut)
    return gain


def centred(rng, dims, deviation, reach, shards=(), dtype=jnp.bfloat16):
    factor_of = levels(rng, dims, shards, -0.22, 0.18) if shards else 1.0
    entries = jax.random.normal(rng, dims, jnp.float32) * deviation * factor_of
    return jnp.minimum(jnp.maximum(entries, -reach), reach).astype(dtype)


def setup_inputs(seed: int = 0) -> dict:
    key_list = jax.random.split(jax.random.key(seed), 8)
    return {
        "queries": draw_queries(jax.random.fold_in(key_list[7], 71), 0),
        "key_vectors": draw_key_vectors(jax.random.fold_in(key_list[7], 71), 0),
        "values": centred(key_list[2], (TICKS + 1, SEQ_TOK, WIDTH), 1.0, 6.0, ((1, 64), (2, 4))),
        "learn_rates": jnp.clip(jnp.exp(math.log(0.01) - 2.30258502 * jax.random.uniform(key_list[3], (TICKS, SEQ_TOK, HEADS), jnp.float32) ** levels(key_list[3], (TICKS, SEQ_TOK, HEADS), ((1, 64), (2, 4)), -0.2, 0.2)), 0.001, 0.01),
        "norm_gain": jnp.clip(1.0 + 0.18 * jax.random.normal(key_list[4], (WIDTH,), jnp.float32), 0.1, 1.9),
        "out_weight": centred(key_list[5], (WIDTH, WIDTH), WIDTH ** -0.5, 0.125, ((0, 4),)),
        "incoming": centred(key_list[6], (N_SEQ, HEADS, 3, HD, HD), HD ** -0.5, 0.25, ((0, 64), (1, 4)), jnp.float32),
    }


def fast_apply(rounded, query_rows):
    first_proj = jnp.dot(query_rows, rounded[0], preferred_element_type=jnp.float32)
    third_proj = jnp.dot(query_rows, rounded[1], preferred_element_type=jnp.float32)
    hidden = (first_proj * jax.nn.sigmoid(first_proj) * third_proj).astype(jnp.bfloat16)
    return jnp.dot(hidden, rounded[2], preferred_element_type=jnp.float32)

def fast_update(fast_state, rounded, key_rows, scaled_values):
    first_proj = jnp.dot(key_rows, rounded[0], preferred_element_type=jnp.float32)
    third_proj = jnp.dot(key_rows, rounded[1], preferred_element_type=jnp.float32)
    gate_sig = jax.nn.sigmoid(first_proj)
    hidden = (first_proj * gate_sig * third_proj).astype(jnp.bfloat16)
    grad_down = jnp.dot(hidden.T, scaled_values, preferred_element_type=jnp.float32)
    back_grad = jnp.dot(scaled_values, rounded[2].T, preferred_element_type=jnp.float32)
    grad_first = (back_grad * third_proj * gate_sig * (1.0 + first_proj * (1.0 - gate_sig))).astype(jnp.bfloat16)
    grad_third = (back_grad * first_proj * gate_sig).astype(jnp.bfloat16)
    grad_one = jnp.dot(key_rows.T, grad_first, preferred_element_type=jnp.float32)
    grad_three = jnp.dot(key_rows.T, grad_third, preferred_element_type=jnp.float32)
    stepped = fast_state + jnp.stack([grad_one, grad_three, grad_down])
    before_sq = lax.optimization_barrier(jnp.mean(fast_state * fast_state, axis=1, keepdims=True))
    after_sq = lax.optimization_barrier(jnp.mean(stepped * stepped, axis=1, keepdims=True))
    return stepped * jnp.sqrt((before_sq + 1e-06) / (after_sq + 1e-06))

def window_attend(query_rows, prior_keys, own_keys, prior_vals, own_vals):
    length = query_rows.shape[0]
    joined_keys = jnp.concatenate([prior_keys, own_keys], axis=0)
    joined_vals = jnp.concatenate([prior_vals, own_vals], axis=0)
    scores = jnp.dot(query_rows, joined_keys.T, preferred_element_type=jnp.float32) * query_rows.shape[1] ** (-0.5)
    query_pos = jnp.arange(length)[:, None] + length
    key_pos = jnp.arange(2 * length)[None, :]
    allowed = (key_pos <= query_pos) & (key_pos > query_pos - length)
    scores = jnp.where(allowed, scores, -1e+30)
    peak = lax.optimization_barrier(jnp.max(scores, axis=1, keepdims=True))
    expo = jnp.exp(scores - peak)
    probs = (expo / lax.optimization_barrier(jnp.sum(expo, axis=1, keepdims=True))).astype(jnp.bfloat16)
    return jnp.dot(probs, joined_vals, preferred_element_type=jnp.float32)

def mix_head(fast_out, attended, gain_row):
    normed = fast_out * lax.rsqrt(lax.optimization_barrier(jnp.mean(fast_out * fast_out, axis=1, keepdims=True)) + 1e-06) * gain_row
    return (attended + normed).astype(jnp.bfloat16)

def one_head(fast_state, query_rows, prior_keys, own_keys, prior_vals, own_vals, rate_rows, gain_row):
    rounded = fast_state.astype(jnp.bfloat16)
    fast_out = fast_apply(rounded, query_rows)
    scaled_values = (rate_rows[:, None] * own_vals.astype(jnp.float32)).astype(jnp.bfloat16)
    updated = fast_update(fast_state, rounded, own_keys, scaled_values)
    attended = window_attend(query_rows, prior_keys, own_keys, prior_vals, own_vals)
    return (mix_head(fast_out, attended, gain_row), updated)

def reference(queries, key_vectors, values, learn_rates, norm_gain, out_weight, incoming):
    query_all = queries.reshape(TICKS, N_SEQ, GROUP, HEADS, HD)
    key_all = key_vectors.reshape(TICKS + 1, N_SEQ, GROUP, HEADS, HD)
    value_all = values.reshape(TICKS + 1, N_SEQ, GROUP, HEADS, HD)
    rate_all = learn_rates.reshape(TICKS, N_SEQ, GROUP, HEADS)
    gains = norm_gain.reshape(HEADS, HD)
    rows_out = out_weight.reshape(HEADS, HD, WIDTH)
    per_head = jax.vmap(one_head, in_axes=(0, 1, 1, 1, 1, 1, 1, 0))

    def one_block(inputs):
        fast_state, query_rows, prior_keys, own_keys, prior_vals, own_vals, rate_rows = inputs
        combined, updated = per_head(fast_state, query_rows, prior_keys, own_keys, prior_vals, own_vals, rate_rows, gains)
        total = jnp.zeros((GROUP, WIDTH), jnp.float32)
        for head_index in range(HEADS):
            partial_value = jnp.dot(combined[head_index], rows_out[head_index], preferred_element_type=jnp.float32).astype(jnp.bfloat16)
            partial_value = lax.optimization_barrier(partial_value)
            total = total + partial_value.astype(jnp.float32)
        return (total.astype(jnp.bfloat16), updated)
    fast_states = incoming
    outputs = []
    for tick_index in range(TICKS):
        mixed, updated = lax.map(one_block, (fast_states, query_all[tick_index], jnp.roll(key_all[tick_index], 1, axis=0), key_all[tick_index + 1], jnp.roll(value_all[tick_index], 1, axis=0), value_all[tick_index + 1], rate_all[tick_index]))
        outputs.append(mixed.reshape(SEQ_TOK, WIDTH))
        if tick_index + 1 < TICKS:
            fast_states = jnp.roll(updated, 1, axis=0)
        else:
            fast_states = updated
    return (jnp.stack(outputs), fast_states)
```

```python
import functools

import jax
import jax.numpy as jnp
from jax import lax
from jax.experimental import pallas as pl
from jax.experimental.pallas import tpu as pltpu
from jax.sharding import PartitionSpec as P

BF = jnp.bfloat16
F32 = jnp.float32
ROWS, HD = 256, 512
EPS = 1e-06
NX, NY, NZH = 4, 4, 4
AXES = ("seq", "head")


def flat(spot):
    zh, y, x, head = spot
    return ((zh % NZH) * NY * NX + (y % NY) * NX + x % NX) * 4 + head


def places():
    return [(zh, y, x, h) for zh in range(NZH) for y in range(NY) for x in range(NX) for h in range(4)]


def target(spot, by):
    zh, y, x, head = spot
    block = (zh * 16 + y * 4 + x + by) % 64
    return (block // 16, block // 4 % 4, block % 4, head)


def crosses(spot, by):
    return target(spot, by)[0] != spot[0]


def moved(spot, dx, dy):
    zh, y, x, head = spot
    return (zh, (y + dy) % NY, (x + dx) % NX, head)


def permute(x, pairs):
    return lax.ppermute(x, AXES, [(flat(a), flat(b)) for a, b in pairs])


def send_direct(x, by):
    return permute(x, [(s, target(s, by)) for s in places()])


def send_relayed(x, by, dx, dy):
    near = permute(x, [(s, target(s, by)) for s in places() if not crosses(s, by)])
    first = permute(x, [(s, moved(s, dx, dy)) for s in places() if crosses(s, by)])
    far = permute(first, [(moved(s, dx, dy), target(s, by)) for s in places() if crosses(s, by)])
    return near, far


def send_late(x, by):
    def inside(s):
        return (s[0],) + target(s, by)[1:]

    near = permute(x, [(s, inside(s)) for s in places()])
    far = permute(near, [(inside(s), target(s, by)) for s in places() if crosses(s, by)])
    return near, far


def from_far(by):
    inner = lax.axis_index("seq") % 16 - by
    return (inner < 0) | (inner >= 16)


def dot(a, b):
    return jnp.dot(a, b, preferred_element_type=F32)


def dot_nt(a, b):
    return lax.dot_general(a, b, (((1,), (1,)), ((), ())), preferred_element_type=F32)


def dot_tn(a, b):
    return lax.dot_general(a, b, (((0,), (0,)), ((), ())), preferred_element_type=F32)


def pick(far, pair):
    if len(pair) == 1:
        return pair[0][...]
    return jnp.where(far, pair[1][...], pair[0][...])


def update(w, r, k, v, rates, store):
    ka = dot(k, r[0])
    kb = dot(k, r[1])
    s = jax.nn.sigmoid(ka)
    kas = ka * s
    kh = (kas * kb).astype(BF)
    sv = (rates * v.astype(F32)).astype(BF)
    bk = dot_nt(sv, r[2])
    d1 = (bk * kb * (s * (1.0 + ka * (1.0 - s)))).astype(BF)
    d3 = (bk * kas).astype(BF)
    for i, (a, b) in enumerate(((k, d1), (k, d3), (kh, sv))):
        for j in range(0, HD, 256):
            cols = slice(j, j + 256)
            old = w(i, cols)
            new = old + dot_tn(a, b[:, cols])
            before = jnp.mean(old * old, axis=0, keepdims=True) + EPS
            after = jnp.mean(new * new, axis=0, keepdims=True) + EPS
            store(i, cols, new * jnp.sqrt(before / after))


def fast_out(r, q, gain):
    qa = dot(q, r[0])
    qb = dot(q, r[1])
    qh = (qa * jax.nn.sigmoid(qa) * qb).astype(BF)
    fo = dot(qh, r[2])
    return fo * lax.rsqrt(jnp.mean(fo * fo, axis=1, keepdims=True) + EPS) * gain


def window(q, kp, k, vp, v):
    scale = HD**-0.5
    row = lax.broadcasted_iota(jnp.int32, (ROWS, ROWS), 0)
    col = lax.broadcasted_iota(jnp.int32, (ROWS, ROWS), 1)
    old = jnp.where(col > row, dot_nt(q, kp) * scale, -1e30)
    own = jnp.where(col <= row, dot_nt(q, k) * scale, -1e30)
    peak = jnp.maximum(jnp.max(old, axis=1, keepdims=True), jnp.max(own, axis=1, keepdims=True))
    old = jnp.exp(old - peak)
    own = jnp.exp(own - peak)
    total = jnp.sum(old, axis=1, keepdims=True) + jnp.sum(own, axis=1, keepdims=True)
    return dot((old / total).astype(BF), vp) + dot((own / total).astype(BF), v)


def project(cm, weight, give, keep):
    head = lax.axis_index("head")
    z_lo, core = head // 2, head % 2
    for out, c in ((give, 1 - core), (keep, core)):
        for i, z in enumerate((z_lo, 1 - z_lo)):
            at = pl.multiple_of((z * 2 + c) * HD, HD)
            out[i] = dot(cm, weight[:, pl.ds(at, HD)]).astype(BF)


def first_tick(u, k, v, rates, q, gain, state, normed):
    r = [u[i].astype(BF) for i in range(3)]

    def store(i, cols, new):
        state[i, :, cols] = new

    update(lambda i, cols: u[i, :, cols], r, k[...], v[...], rates[...], store)
    normed[...] = fast_out(r, q[...], gain[...])


def second_update(u, k, vn, vf, rates, w1, w3, w2):
    far = from_far(-1)
    r = [u[i].astype(BF) for i in range(3)]
    outs = (w1, w3, w2)

    def store(i, cols, new):
        outs[i][:, cols] = new.astype(BF)

    update(lambda i, cols: u[i, :, cols], r, k[...], pick(far, (vn, vf)), rates[...], store)


def second_mix(u, q, kp, vp, k, vn, vf, gain, cm):
    far = from_far(-1)
    r = [u[i].astype(BF) for i in range(3)]
    att = window(q[...], kp[...], k[...], vp[...], pick(far, (vn, vf)))
    cm[...] = (att + fast_out(r, q[...], gain[...])).astype(BF)


def first_mix(q, kvn, kvf, k, v, normed, weight, give, keep):
    far = from_far(1)
    kv = pick(far, (kvn, kvf))
    cm = (window(q[...], kv[0], k[...], kv[1], v[...]) + normed[...]).astype(BF)
    project(cm, weight, give, keep)


def project_only(cm, weight, give, keep):
    project(cm[...], weight, give, keep)


def attend(q, kvn, kvf, k, v, att):
    far = from_far(1)
    kv = pick(far, (kvn, kvf))
    att[...] = window(q[...], kv[0], k[...], kv[1], v[...])


def third_mix(w1n, w1f, w3, w2n, w2f, q, att, gain, weight, give, keep, m1, m3, m2):
    far = from_far(2)
    r = [pick(far, (w1n, w1f)), w3[...], pick(far, (w2n, w2f))]
    for m, x in zip((m1, m3, m2), r):
        m[...] = x
    cm = (att[...] + fast_out(r, q[...], gain[...])).astype(BF)
    project(cm, weight, give, keep)


def third_update(m1, m3, m2, k, v, rates, out):
    ms = (m1, m3, m2)

    def store(i, cols, new):
        out[i, :, cols] = new

    update(lambda i, cols: ms[i][:, cols].astype(F32), [m[...] for m in ms], k[...], v[...], rates[...], store)


def call(body, outs, args, matmuls):
    whole = pl.BlockSpec(memory_space=pltpu.VMEM)
    size = sum(a.size * a.dtype.itemsize for a in args)
    return pl.pallas_call(
        body,
        out_shape=[jax.ShapeDtypeStruct(s, d) for s, d in outs],
        in_specs=[whole] * len(args),
        out_specs=[whole] * len(outs),
        compiler_params=pltpu.CompilerParams(vmem_limit_bytes=40 * 1024 * 1024),
        cost_estimate=pl.CostEstimate(flops=matmuls * 2 * ROWS * HD * HD * 2, bytes_accessed=size, transcendentals=ROWS * HD),
    )(*args)


PAIR = ((2, ROWS, HD), BF)
FLAT = ((ROWS, HD), BF)
SQUARE = ((HD, HD), BF)
STATE = ((3, HD, HD), F32)


def head_sum(give, keep):
    spots = places()
    got = permute(give, [(s, s[:3] + (s[3] ^ 1,)) for s in spots])
    pair = got.astype(F32) + keep.astype(F32)
    other = permute(pair[1].astype(BF), [(s, s[:3] + (s[3] ^ 2,)) for s in spots])
    return (pair[0] + other.astype(F32)).astype(BF)


def after(x, y):
    return lax.optimization_barrier((x, y))[0]


def on_device(queries, keys, values, rates, gain, weight, incoming):
    gain = gain.reshape(1, HD)
    u0 = incoming[0, 0]
    q = [queries[t] for t in range(3)]
    k = [keys[t] for t in range(4)]
    v = [values[t] for t in range(4)]

    k2b = send_direct(k[2], -1)
    v2n, v2f = send_late(v[2], -1)
    r1b = send_direct(rates[1].reshape(2, 128), -1).reshape(ROWS, 1)
    kv0 = send_relayed(jnp.stack([k[0], v[0]]), 1, 1, 0)
    kv2 = send_late(jnp.stack([k[2], v[2]]), 1)
    q1b = send_direct(after(q[1], k2b), -1)

    state, normed0 = call(first_tick, [STATE, ((ROWS, HD), F32)], (u0, k[1], v[1], rates[0], q[0], gain), 9)
    w1, w3, w2 = call(second_update, [SQUARE] * 3, (state, k2b, v2n, v2f, r1b), 6)
    w3 = send_direct(w3, 2)
    w1 = send_relayed(w1, 2, 0, 1)
    w2 = send_relayed(w2, 2, 0, -1)
    (cm1,) = call(second_mix, [FLAT], (state, q1b, k[1], v[1], k2b, v2n, v2f, gain), 5)
    cm1 = send_direct(cm1, 1)
    give0, keep0 = call(first_mix, [PAIR] * 2, (q[0], *kv0, k[1], v[1], normed0, weight), 6)
    (att2,) = call(attend, [((ROWS, HD), F32)], (q[2], *kv2, k[3], v[3]), 2)
    out0 = head_sum(give0, keep0)
    give1, keep1 = call(project_only, [PAIR] * 2, (cm1, weight), 4)
    out1 = head_sum(give1, keep1)
    give2, keep2, m1, m3, m2 = call(third_mix, [PAIR] * 2 + [SQUARE] * 3, (*w1, w3, *w2, q[2], att2, gain, weight), 7)
    out2 = head_sum(give2, keep2)
    (outgoing,) = call(third_update, [STATE], (m1, m3, m2, k[3], v[3], rates[2]), 6)
    return jnp.stack([out0, out1, out2]), outgoing[None, None]


def solution(mesh):
    placed = (
        P(None, "seq", "head"),
        P(None, "seq", "head"),
        P(None, "seq", "head"),
        P(None, "seq", "head"),
        P("head"),
        P("head", None),
        P("seq", "head", None, None, None),
    )
    return jax.shard_map(
        on_device,
        mesh=mesh,
        in_specs=placed,
        out_specs=(P(None, "seq", "head"), P("seq", "head", None, None, None)),
        check_vma=False,
    )
```

```python
import functools

import jax
import jax.numpy as jnp
from jax import lax
from jax.experimental import pallas as pl
from jax.experimental.pallas import tpu as pltpu
from jax.sharding import PartitionSpec as P

BF = jnp.bfloat16
F32 = jnp.float32
ROWS, HD = 256, 512
EPS = 1e-06
NX, NY, NZH = 4, 4, 4
AXES = ("seq", "head")


def flat(spot):
    zh, y, x, head = spot
    return ((zh % NZH) * NY * NX + (y % NY) * NX + x % NX) * 4 + head


def places():
    return [(zh, y, x, h) for zh in range(NZH) for y in range(NY) for x in range(NX) for h in range(4)]


def target(spot, by):
    zh, y, x, head = spot
    block = (zh * 16 + y * 4 + x + by) % 64
    return (block // 16, block // 4 % 4, block % 4, head)


def crosses(spot, by):
    return target(spot, by)[0] != spot[0]


def moved(spot, dx, dy):
    zh, y, x, head = spot
    return (zh, (y + dy) % NY, (x + dx) % NX, head)


def permute(x, pairs):
    return lax.ppermute(x, AXES, [(flat(a), flat(b)) for a, b in pairs])


def send_direct(x, by):
    return permute(x, [(s, target(s, by)) for s in places()])


def send_near(x, by):
    return permute(x, [(s, target(s, by)) for s in places() if not crosses(s, by)])


def send_first(x, by, dx, dy):
    return permute(x, [(s, moved(s, dx, dy)) for s in places() if crosses(s, by)])


def send_far(x, by, dx, dy):
    return permute(x, [(moved(s, dx, dy), target(s, by)) for s in places() if crosses(s, by)])


def send_late(x, by):
    def inside(s):
        return (s[0],) + target(s, by)[1:]

    near = permute(x, [(s, inside(s)) for s in places()])
    return near, [(inside(s), target(s, by)) for s in places() if crosses(s, by)]


def from_far(by):
    inner = lax.axis_index("seq") % 16 - by
    return (inner < 0) | (inner >= 16)


def dot(a, b):
    return jnp.dot(a, b, preferred_element_type=F32)


def dot_nt(a, b):
    return lax.dot_general(a, b, (((1,), (1,)), ((), ())), preferred_element_type=F32)


def dot_tn(a, b):
    return lax.dot_general(a, b, (((0,), (0,)), ((), ())), preferred_element_type=F32)


def column(row):
    eye = lax.broadcasted_iota(jnp.int32, (ROWS, ROWS), 0) == lax.broadcasted_iota(jnp.int32, (ROWS, ROWS), 1)
    return jnp.sum(jnp.where(eye, row, 0.0), axis=1, keepdims=True)


def update(w, r, k, v, rates, store):
    ka = dot(k, r[0])
    kb = dot(k, r[1])
    s = jax.nn.sigmoid(ka)
    kas = ka * s
    kh = (kas * kb).astype(BF)
    sv = (rates * v.astype(F32)).astype(BF)
    bk = dot_nt(sv, r[2])
    d1 = (bk * kb * (s * (1.0 + ka * (1.0 - s)))).astype(BF)
    d3 = (bk * kas).astype(BF)
    for i, (a, b) in enumerate(((k, d1), (k, d3), (kh, sv))):
        for j in range(0, HD, 256):
            cols = slice(j, j + 256)
            old = w(i, cols)
            new = old + dot_tn(a, b[:, cols])
            before = jnp.mean(old * old, axis=0, keepdims=True) + EPS
            after = jnp.mean(new * new, axis=0, keepdims=True) + EPS
            store(i, cols, new * jnp.sqrt(before / after))


def fast_out(r, q, gain):
    qa = dot(q, r[0])
    qb = dot(q, r[1])
    qh = (qa * jax.nn.sigmoid(qa) * qb).astype(BF)
    fo = dot(qh, r[2])
    return fo * lax.rsqrt(jnp.mean(fo * fo, axis=1, keepdims=True) + EPS) * gain


def window(q, kp, k, vp, v):
    scale = HD**-0.5
    row = lax.broadcasted_iota(jnp.int32, (ROWS, ROWS), 0)
    col = lax.broadcasted_iota(jnp.int32, (ROWS, ROWS), 1)
    old = jnp.where(col > row, dot_nt(q, kp) * scale, -1e30)
    own = jnp.where(col <= row, dot_nt(q, k) * scale, -1e30)
    peak = jnp.maximum(jnp.max(old, axis=1, keepdims=True), jnp.max(own, axis=1, keepdims=True))
    old = jnp.exp(old - peak)
    own = jnp.exp(own - peak)
    total = jnp.sum(old, axis=1, keepdims=True) + jnp.sum(own, axis=1, keepdims=True)
    return dot((old / total).astype(BF), vp) + dot((own / total).astype(BF), v)


def project(cm, weight, give, own, far):
    head = lax.axis_index("head")
    z_lo, core = head // 2, head % 2

    def part(z, c):
        at = pl.multiple_of((z * 2 + c) * HD, HD)
        return dot(cm, weight[:, pl.ds(at, HD)]).astype(BF)

    give[1] = part(1 - z_lo, 1 - core)
    give[0] = part(z_lo, 1 - core)
    far[...] = part(1 - z_lo, core)
    own[...] = part(z_lo, core)


def pack_pair(keys, values, out, sems):
    copies = [pltpu.make_async_copy(a.at[2], out.at[i], sems.at[i]) for i, a in enumerate((keys, values))]
    for c in copies:
        c.start()
    for c in copies:
        c.wait()


def pack_rest(keys, values, queries, _, out, q1, sems):
    copies = [pltpu.make_async_copy(a.at[0], out.at[i], sems.at[i]) for i, a in enumerate((keys, values))]
    copies.append(pltpu.make_async_copy(queries.at[1], q1, sems.at[2]))
    for c in copies:
        c.start()
    for c in copies:
        c.wait()


def first_tick(u, k, v, rates, q, gain, state, normed):
    r = [u[0, 0, i].astype(BF) for i in range(3)]

    def store(i, cols, new):
        state[i, :, cols] = new

    update(lambda i, cols: u[0, 0, i, :, cols], r, k[0], v[0], column(rates[0]), store)
    normed[...] = fast_out(r, q[0], gain[...])


def second_update(u, kv, rates, *pieces):
    r = [u[i].astype(BF) for i in range(3)]

    def store(i, cols, new):
        new = new.astype(BF)
        start = 0
        for piece, rows in zip(pieces, PIECES):
            low, high = max(start, i * HD), min(start + rows, (i + 1) * HD)
            if low < high:
                piece[low - start : high - start, cols] = new[low - i * HD : high - i * HD]
            start += rows

    update(lambda i, cols: u[i, :, cols], r, kv[0], kv[1], column(rates[1]), store)


def second_mix(u, qn, qf, kp, vp, kv, gain, cm):
    q = jnp.where(from_far(-1), qf[...], qn[...])
    r = [u[i].astype(BF) for i in range(3)]
    att = window(q, kp[0], kv[0], vp[0], kv[1])
    cm[...] = (att + fast_out(r, q, gain[...])).astype(BF)


def first_mix(q, kvn, kvf, k, v, normed, weight, give, own, far):
    late = from_far(1)
    kp = jnp.where(late, kvf[0], kvn[0])
    vp = jnp.where(late, kvf[1], kvn[1])
    cm = (window(q[0], kp, k[0], vp, v[0]) + normed[...]).astype(BF)
    project(cm, weight, give, own, far)


def project_only(cm, weight, give, own, far):
    project(cm[...], weight, give, own, far)


def attend(q, kv, k, v, att):
    att[...] = window(q[0], kv[0], k[0], kv[1], v[0])


def third_mix(a, bn, bf, cn, cf, q, att, gain, weight, give, own, far, m):
    late = from_far(2)
    one, two = PIECES[0], PIECES[0] + PIECES[1]
    m[:one] = a[...]
    m[one:two] = jnp.where(late, bf[...], bn[...])
    m[two:] = jnp.where(late, cf[...], cn[...])
    r = [m[i * HD : (i + 1) * HD] for i in range(3)]
    cm = (att[...] + fast_out(r, q[0], gain[...])).astype(BF)
    project(cm, weight, give, own, far)


def third_update(m, k, v, rates, out):
    def store(i, cols, new):
        out[0, 0, i, :, cols] = new

    r = [m[i * HD : (i + 1) * HD] for i in range(3)]
    update(lambda i, cols: m[i * HD : (i + 1) * HD, cols].astype(F32), r, k[0], v[0], column(rates[2]), store)


def first_two(other0, got0, own0, other1, got1, own1, out):
    out[0] = (got0[0].astype(F32) + own0[...].astype(F32) + other0[...].astype(F32)).astype(BF)
    out[1] = (got1[0].astype(F32) + own1[...].astype(F32) + other1[...].astype(F32)).astype(BF)


def last_one(_, other, got, own, out):
    out[0] = (got[0].astype(F32) + own[...].astype(F32) + other[...].astype(F32)).astype(BF)


PIECES = (576, 480, 480)
WHOLE = pl.BlockSpec(memory_space=pltpu.VMEM)
HBM = pl.BlockSpec(memory_space=pl.ANY)


def slab(shape, index):
    return pl.BlockSpec(shape, lambda _, index=index: (index,) + (0,) * (len(shape) - 1))


def rows_of(t):
    return slab((1, ROWS, HD), t)


def call(body, outs, args, matmuls=0, scratch=(), **more):
    size = sum(a.size * a.dtype.itemsize for a, _ in args)
    return pl.pallas_call(
        body,
        out_shape=[jax.ShapeDtypeStruct(s, d) for s, d, _ in outs],
        grid=(1,),
        in_specs=[s for _, s in args],
        out_specs=[s for _, _, s in outs],
        scratch_shapes=list(scratch),
        compiler_params=pltpu.CompilerParams(vmem_limit_bytes=32 * 1024 * 1024),
        cost_estimate=pl.CostEstimate(flops=matmuls * 2 * ROWS * HD * HD * 2, bytes_accessed=size, transcendentals=ROWS * HD),
        **more,
    )(*[a for a, _ in args])


FLAT = ((ROWS, HD), BF, WHOLE)
WIDE = ((ROWS, HD), F32, WHOLE)
SUM = [((2, ROWS, HD), BF, WHOLE), FLAT, FLAT]
STATE = ((3, HD, HD), F32, WHOLE)


def head_sum(give, own, far):
    spots = places()
    got = permute(give, [(s, s[:3] + (s[3] ^ 1,)) for s in spots])
    pair = (got[1].astype(F32) + far.astype(F32)).astype(BF)
    other = permute(pair, [(s, s[:3] + (s[3] ^ 2,)) for s in spots])
    return (other, WHOLE), (got, WHOLE), (own, WHOLE)


def after(x, *ys):
    return lax.optimization_barrier((x,) + ys)[0]


def on_device(queries, keys, values, rates, gain, weight, incoming):
    gain = gain.reshape(1, HD)
    rates = rates.reshape(3, 1, ROWS)
    rate = (rates, slab((3, 1, ROWS), 0))
    gain = (gain, slab((1, HD), 0))
    weight = (weight, slab((HD, 4 * HD), 0))

    (kv2,) = call(pack_pair, [((2, ROWS, HD), BF, HBM)], ((keys, HBM), (values, HBM)), scratch=[pltpu.SemaphoreType.DMA((2,))])
    kv0, q1 = call(
        pack_rest,
        [((2, ROWS, HD), BF, HBM), ((ROWS, HD), BF, HBM)],
        ((keys, HBM), (values, HBM), (queries, HBM), (kv2, HBM)),
        scratch=[pltpu.SemaphoreType.DMA((3,))],
    )
    next_rates = send_direct(rates, -1)
    next_kv = send_direct(kv2, -1)
    q1n, q1_pairs = send_late(q1, -1)
    kv2 = send_direct(kv2, 1)
    kv0n, kv0_pairs = send_late(kv0, 1)

    state, normed0 = call(
        first_tick,
        [STATE, WIDE],
        (
            (incoming, slab((1, 1, 3, HD, HD), 0)),
            (keys, rows_of(1)),
            (values, rows_of(1)),
            rate,
            (queries, rows_of(0)),
            gain,
        ),
        9,
    )
    a, b, c = call(
        second_update,
        [((n, HD), BF, WHOLE) for n in PIECES],
        ((state, WHOLE), (next_kv, WHOLE), (next_rates, WHOLE)),
        6,
    )
    b1, c1 = send_first(b, 2, 0, 1), send_first(c, 2, 0, -1)
    a2, bn, cn = send_direct(a, 2), send_near(b, 2), send_near(c, 2)
    q1f = permute(after(q1n, a), q1_pairs)
    (cm1,) = call(
        second_mix,
        [FLAT],
        ((state, WHOLE), (q1n, WHOLE), (q1f, WHOLE), (keys, rows_of(1)), (values, rows_of(1)), (next_kv, WHOLE), gain),
        5,
    )
    kv0f = permute(after(kv0n, cm1), kv0_pairs)
    bf, cf = send_far(after(b1, cm1), 2, 0, 1), send_far(after(c1, cm1), 2, 0, -1)
    cm1 = send_direct(cm1, 1)
    sum0 = call(
        first_mix,
        SUM,
        ((queries, rows_of(0)), (kv0n, WHOLE), (kv0f, WHOLE), (keys, rows_of(1)), (values, rows_of(1)), (normed0, WHOLE), weight),
        6,
    )
    (att2,) = call(attend, [WIDE], ((queries, rows_of(2)), (kv2, WHOLE), (keys, rows_of(3)), (values, rows_of(3))), 2)
    sum0 = head_sum(*sum0)
    sum1 = head_sum(*call(project_only, SUM, ((cm1, WHOLE), weight), 4))
    (mixed,) = call(first_two, [((3, ROWS, HD), BF, slab((3, ROWS, HD), 0))], sum0 + sum1)
    *sum2, m = call(
        third_mix,
        SUM + [((3 * HD, HD), BF, WHOLE)],
        (
            (a2, WHOLE),
            (bn, WHOLE),
            (bf, WHOLE),
            (cn, WHOLE),
            (cf, WHOLE),
            (queries, rows_of(2)),
            (att2, WHOLE),
            gain,
            weight,
        ),
        7,
    )
    sum2 = head_sum(*sum2)
    (outgoing,) = call(
        third_update,
        [((1, 1, 3, HD, HD), F32, slab((1, 1, 3, HD, HD), 0))],
        ((m, WHOLE), (keys, rows_of(3)), (values, rows_of(3)), rate),
        6,
    )
    (mixed,) = call(
        last_one, [((3, ROWS, HD), BF, rows_of(2))], ((mixed, HBM),) + sum2, input_output_aliases={0: 0}
    )
    return mixed, outgoing


def solution(mesh):
    placed = (
        P(None, "seq", "head"),
        P(None, "seq", "head"),
        P(None, "seq", "head"),
        P(None, "seq", "head"),
        P("head"),
        P("head", None),
        P("seq", "head", None, None, None),
    )
    return jax.shard_map(
        on_device,
        mesh=mesh,
        in_specs=placed,
        out_specs=(P(None, "seq", "head"), P("seq", "head", None, None, None)),
        check_vma=False,
    )
```

```python
import functools

import jax
import jax.numpy as jnp
from jax import lax
from jax.experimental import pallas as pl
from jax.experimental.pallas import tpu as pltpu
from jax.sharding import PartitionSpec as P

BF = jnp.bfloat16
F32 = jnp.float32
ROWS, HD = 256, 512
EPS = 1e-06
NX, NY, NZH = 4, 4, 4
AXES = ("seq", "head")


def flat(spot):
    zh, y, x, head = spot
    return ((zh % NZH) * NY * NX + (y % NY) * NX + x % NX) * 4 + head


def places():
    return [(zh, y, x, h) for zh in range(NZH) for y in range(NY) for x in range(NX) for h in range(4)]


def target(spot, by):
    zh, y, x, head = spot
    block = (zh * 16 + y * 4 + x + by) % 64
    return (block // 16, block // 4 % 4, block % 4, head)


def crosses(spot, by):
    return target(spot, by)[0] != spot[0]


def moved(spot, dx, dy):
    zh, y, x, head = spot
    return (zh, (y + dy) % NY, (x + dx) % NX, head)


def permute(x, pairs):
    return lax.ppermute(x, AXES, [(flat(a), flat(b)) for a, b in pairs])


def send_direct(x, by):
    return permute(x, [(s, target(s, by)) for s in places()])


def send_near(x, by):
    return permute(x, [(s, target(s, by)) for s in places() if not crosses(s, by)])


def send_first(x, by, dx, dy):
    return permute(x, [(s, moved(s, dx, dy)) for s in places() if crosses(s, by)])


def send_far(x, by, dx, dy):
    return permute(x, [(moved(s, dx, dy), target(s, by)) for s in places() if crosses(s, by)])


def send_late(x, by):
    def inside(s):
        return (s[0],) + target(s, by)[1:]

    near = permute(x, [(s, inside(s)) for s in places()])
    return near, [(inside(s), target(s, by)) for s in places() if crosses(s, by)]


def from_far(by):
    inner = lax.axis_index("seq") % 16 - by
    return (inner < 0) | (inner >= 16)


def dot(a, b):
    return jnp.dot(a, b, preferred_element_type=F32)


def dot_nt(a, b):
    return lax.dot_general(a, b, (((1,), (1,)), ((), ())), preferred_element_type=F32)


def dot_tn(a, b):
    return lax.dot_general(a, b, (((0,), (0,)), ((), ())), preferred_element_type=F32)


def column(row):
    eye = lax.broadcasted_iota(jnp.int32, (ROWS, ROWS), 0) == lax.broadcasted_iota(jnp.int32, (ROWS, ROWS), 1)
    return jnp.sum(jnp.where(eye, row, 0.0), axis=1, keepdims=True)


def update(w, r, k, v, rates, store):
    ka = dot(k, r[0])
    kb = dot(k, r[1])
    s = jax.nn.sigmoid(ka)
    kas = ka * s
    kh = (kas * kb).astype(BF)
    sv = (rates * v.astype(F32)).astype(BF)
    bk = dot_nt(sv, r[2])
    d1 = (bk * kb * (s * (1.0 + ka * (1.0 - s)))).astype(BF)
    d3 = (bk * kas).astype(BF)
    for i, (a, b) in enumerate(((k, d1), (k, d3), (kh, sv))):
        for j in range(0, HD, 256):
            cols = slice(j, j + 256)
            old = w(i, cols)
            new = old + dot_tn(a, b[:, cols])
            before = jnp.mean(old * old, axis=0, keepdims=True) + EPS
            after = jnp.mean(new * new, axis=0, keepdims=True) + EPS
            store(i, cols, new * jnp.sqrt(before / after))


def fast_out(r, q, gain):
    qa = dot(q, r[0])
    qb = dot(q, r[1])
    qh = (qa * jax.nn.sigmoid(qa) * qb).astype(BF)
    fo = dot(qh, r[2])
    return fo * lax.rsqrt(jnp.mean(fo * fo, axis=1, keepdims=True) + EPS) * gain


def window(q, kp, k, vp, v):
    scale = HD**-0.5
    row = lax.broadcasted_iota(jnp.int32, (ROWS, ROWS), 0)
    col = lax.broadcasted_iota(jnp.int32, (ROWS, ROWS), 1)
    old = jnp.where(col > row, dot_nt(q, kp) * scale, -1e30)
    own = jnp.where(col <= row, dot_nt(q, k) * scale, -1e30)
    peak = jnp.maximum(jnp.max(old, axis=1, keepdims=True), jnp.max(own, axis=1, keepdims=True))
    old = jnp.exp(old - peak)
    own = jnp.exp(own - peak)
    total = jnp.sum(old, axis=1, keepdims=True) + jnp.sum(own, axis=1, keepdims=True)
    return dot((old / total).astype(BF), vp) + dot((own / total).astype(BF), v)


def project(cm, weight, give, own, far):
    head = lax.axis_index("head")
    z_lo, core = head // 2, head % 2

    def part(z, c):
        at = pl.multiple_of((z * 2 + c) * HD, HD)
        return dot(cm, weight[:, pl.ds(at, HD)]).astype(BF)

    give[1] = part(1 - z_lo, 1 - core)
    give[0] = part(z_lo, 1 - core)
    far[...] = part(1 - z_lo, core)
    own[...] = part(z_lo, core)


def pack_pair(keys, values, out, sems):
    copies = [pltpu.make_async_copy(a.at[2], out.at[i], sems.at[i]) for i, a in enumerate((keys, values))]
    for c in copies:
        c.start()
    for c in copies:
        c.wait()


def pack_rest(keys, values, queries, _, out, q1, sems):
    copies = [pltpu.make_async_copy(a.at[0], out.at[i], sems.at[i]) for i, a in enumerate((keys, values))]
    copies.append(pltpu.make_async_copy(queries.at[1], q1, sems.at[2]))
    for c in copies:
        c.start()
    for c in copies:
        c.wait()


def first_tick(u, k, v, rates, q, gain, state, normed):
    r = [u[0, 0, i].astype(BF) for i in range(3)]

    def store(i, cols, new):
        state[i, :, cols] = new

    update(lambda i, cols: u[0, 0, i, :, cols], r, k[0], v[0], column(rates[0]), store)
    normed[...] = fast_out(r, q[0], gain[...])


def second_tick(u, kv, rates, qn, qf, kp, vp, held, gain, one, rest, third, relay, cm):
    r = [u[i].astype(BF) for i in range(3)]

    def store(i, cols, new):
        new = new.astype(BF)
        if i == 0:
            one[:, cols] = new
        else:
            rest[(i - 1) * HD : i * HD, cols] = new
        if i == 2:
            third[:, cols] = new

    update(lambda i, cols: u[i, :, cols], r, kv[0], kv[1], column(rates[1]), store)
    first = lax.axis_index("seq") % 16 == 0
    for i in range(2):
        half = slice(i * ROWS, (i + 1) * ROWS)
        relay[half] = jnp.where(first, held[i], rest[half])
    q = jnp.where(from_far(-1), qf[...], qn[...])
    cm[...] = (window(q, kp[0], kv[0], vp[0], kv[1]) + fast_out(r, q, gain[...])).astype(BF)


def first_mix(q, kv, k, v, normed, weight, give, own, far):
    cm = (window(q[0], kv[0], k[0], kv[1], v[0]) + normed[...]).astype(BF)
    project(cm, weight, give, own, far)


def second_project(cm, weight, give, own, far):
    project(cm[...], weight, give, own, far)


def attend(q, kvn, kvf, k, v, att):
    late = from_far(1)
    kp = jnp.where(late, kvf[:ROWS], kvn[0])
    vp = jnp.where(late, kvf[ROWS:], kvn[1])
    att[...] = window(q[0], kp, k[0], vp, v[0])


def third_mix(a, near, bf, cf, q, att, gain, weight, give, own, far, m):
    late = from_far(2)
    m[:HD] = a[...]
    m[HD : 2 * HD] = jnp.where(late, bf[...], near[:HD])
    m[2 * HD :] = jnp.where(late, cf[...], near[HD:])
    r = [m[i * HD : (i + 1) * HD] for i in range(3)]
    cm = (att[...] + fast_out(r, q[0], gain[...])).astype(BF)
    project(cm, weight, give, own, far)


def third_update(m, k, v, rates, out):
    def store(i, cols, new):
        out[0, 0, i, :, cols] = new

    r = [m[i * HD : (i + 1) * HD] for i in range(3)]
    update(lambda i, cols: m[i * HD : (i + 1) * HD, cols].astype(F32), r, k[0], v[0], column(rates[2]), store)


def first_two(other0, got0, own0, other1, got1, own1, out):
    out[0] = (got0[0].astype(F32) + own0[...].astype(F32) + other0[...].astype(F32)).astype(BF)
    out[1] = (got1[0].astype(F32) + own1[...].astype(F32) + other1[...].astype(F32)).astype(BF)


def last_one(_, other, got, own, out):
    out[0] = (got[0].astype(F32) + own[...].astype(F32) + other[...].astype(F32)).astype(BF)


LEAD = 40 * 10**9
WHOLE = pl.BlockSpec(memory_space=pltpu.VMEM)
HBM = pl.BlockSpec(memory_space=pl.ANY)


def slab(shape, index):
    return pl.BlockSpec(shape, lambda _, index=index: (index,) + (0,) * (len(shape) - 1))


def rows_of(t):
    return slab((1, ROWS, HD), t)


def call(body, outs, args, matmuls=0, scratch=(), lead=0, **more):
    return pl.pallas_call(
        body,
        out_shape=[jax.ShapeDtypeStruct(s, d) for s, d, _ in outs],
        grid=(1,),
        in_specs=[s for _, s in args],
        out_specs=[s for _, _, s in outs],
        scratch_shapes=list(scratch),
        compiler_params=pltpu.CompilerParams(vmem_limit_bytes=32 * 1024 * 1024),
        cost_estimate=pl.CostEstimate(flops=1024 * matmuls + lead, bytes_accessed=1024, transcendentals=0),
        **more,
    )(*[a for a, _ in args])


FLAT = ((ROWS, HD), BF, WHOLE)
WIDE = ((ROWS, HD), F32, WHOLE)
SUM = [((2, ROWS, HD), BF, WHOLE), FLAT, FLAT]
HALF = ((HD, HD), BF, WHOLE)
STATE = ((3, HD, HD), F32, WHOLE)


def head_sum(give, own, far):
    spots = places()
    got = permute(give, [(s, s[:3] + (s[3] ^ 1,)) for s in spots])
    pair = (got[..., 1, :, :].astype(F32) + far.astype(F32)).astype(BF)
    other = permute(pair, [(s, s[:3] + (s[3] ^ 2,)) for s in spots])
    return (other, WHOLE), (got, WHOLE), (own, WHOLE)


def after(x, *ys):
    return lax.optimization_barrier((x,) + ys)[0]


def on_device(queries, keys, values, rates, gain, weight, incoming):
    gain = gain.reshape(1, HD)
    rates = rates.reshape(3, 1, ROWS)
    rate = (rates, slab((3, 1, ROWS), 0))
    gain = (gain, slab((1, HD), 0))
    weight = (weight, slab((HD, 4 * HD), 0))

    (kv2,) = call(pack_pair, [((2, ROWS, HD), BF, HBM)], ((keys, HBM), (values, HBM)), scratch=[pltpu.SemaphoreType.DMA((2,))])
    kv0, q1 = call(
        pack_rest,
        [((2, ROWS, HD), BF, HBM), ((ROWS, HD), BF, HBM)],
        ((keys, HBM), (values, HBM), (queries, HBM), (kv2, HBM)),
        scratch=[pltpu.SemaphoreType.DMA((3,))],
    )
    next_rates = send_direct(rates, -1)
    next_kv = send_direct(kv2, -1)
    q1n, q1_pairs = send_late(q1, -1)
    kv2n, kv2_pairs = send_late(kv2, 1)
    q1f = permute(q1n, q1_pairs)
    kv0 = send_direct(kv0, 1)

    state, normed0 = call(
        first_tick,
        [STATE, WIDE],
        (
            (after(incoming, next_rates, q1n), slab((1, 1, 3, HD, HD), 0)),
            (keys, rows_of(1)),
            (values, rows_of(1)),
            rate,
            (queries, rows_of(0)),
            gain,
        ),
        9,
        lead=LEAD,
    )
    a, bc, c, b, cm1 = call(
        second_tick,
        [HALF, ((2 * HD, HD), BF, WHOLE), HALF, HALF, FLAT],
        (
            (state, WHOLE),
            (next_kv, WHOLE),
            (next_rates, WHOLE),
            (q1n, WHOLE),
            (q1f, WHOLE),
            (keys, rows_of(1)),
            (values, rows_of(1)),
            (kv2n, WHOLE),
            gain,
        ),
        11,
    )
    c1 = send_first(c, 2, 0, -1)
    b1 = permute(b, [(s, moved(s, 0, 1)) for s in places() if crosses(s, 2)] + kv2_pairs)
    a2, near = send_direct(a, 2), send_near(bc, 2)
    bf, cf = send_far(b1, 2, 0, 1), send_far(c1, 2, 0, -1)
    sum0 = head_sum(
        *call(
            first_mix,
            SUM,
            ((queries, rows_of(0)), (after(kv0, q1f), WHOLE), (keys, rows_of(1)), (values, rows_of(1)), (normed0, WHOLE), weight),
            6,
        )
    )
    cm1 = send_direct(after(cm1, b1, c1, sum0[0][0]), 1)
    (att2,) = call(
        attend, [WIDE], ((queries, rows_of(2)), (kv2n, WHOLE), (b1, WHOLE), (keys, rows_of(3)), (values, rows_of(3))), 2
    )
    sum1 = head_sum(*call(second_project, SUM, ((after(cm1, a2, att2), WHOLE), weight), 4))
    (mixed,) = call(first_two, [((3, ROWS, HD), BF, slab((3, ROWS, HD), 0))], sum0 + sum1)
    *sum2, m = call(
        third_mix,
        SUM + [((3 * HD, HD), BF, WHOLE)],
        (
            (a2, WHOLE),
            (near, WHOLE),
            (bf, WHOLE),
            (cf, WHOLE),
            (queries, rows_of(2)),
            (att2, WHOLE),
            gain,
            weight,
        ),
        7,
    )
    sum2 = head_sum(*sum2)
    (outgoing,) = call(
        third_update,
        [((1, 1, 3, HD, HD), F32, slab((1, 1, 3, HD, HD), 0))],
        ((m, WHOLE), (keys, rows_of(3)), (values, rows_of(3)), rate),
        6,
    )
    (mixed,) = call(
        last_one, [((3, ROWS, HD), BF, rows_of(2))], ((mixed, HBM),) + sum2, input_output_aliases={0: 0}
    )
    return mixed, outgoing


def solution(mesh):
    placed = (
        P(None, "seq", "head"),
        P(None, "seq", "head"),
        P(None, "seq", "head"),
        P(None, "seq", "head"),
        P("head"),
        P("head", None),
        P("seq", "head", None, None, None),
    )
    return jax.shard_map(
        on_device,
        mesh=mesh,
        in_specs=placed,
        out_specs=(P(None, "seq", "head"), P("seq", "head", None, None, None)),
        check_vma=False,
    )
```

```python
import functools

import jax
import jax.numpy as jnp
from jax import lax
from jax.experimental import pallas as pl
from jax.experimental.pallas import tpu as pltpu
from jax.sharding import PartitionSpec as P

BF = jnp.bfloat16
F32 = jnp.float32
ROWS, HD = 256, 512
EPS = 1e-06
NX, NY, NZH = 4, 4, 4
AXES = ("seq", "head")


def flat(spot):
    zh, y, x, head = spot
    return ((zh % NZH) * NY * NX + (y % NY) * NX + x % NX) * 4 + head


def places():
    return [(zh, y, x, h) for zh in range(NZH) for y in range(NY) for x in range(NX) for h in range(4)]


def target(spot, by):
    zh, y, x, head = spot
    block = (zh * 16 + y * 4 + x + by) % 64
    return (block // 16, block // 4 % 4, block % 4, head)


def crosses(spot, by):
    return target(spot, by)[0] != spot[0]


def moved(spot, dx, dy):
    zh, y, x, head = spot
    return (zh, (y + dy) % NY, (x + dx) % NX, head)


def permute(x, pairs):
    return lax.ppermute(x, AXES, [(flat(a), flat(b)) for a, b in pairs])


def send_direct(x, by):
    return permute(x, [(s, target(s, by)) for s in places()])


def send_near(x, by):
    return permute(x, [(s, target(s, by)) for s in places() if not crosses(s, by)])


def send_first(x, by, dx, dy):
    return permute(x, [(s, moved(s, dx, dy)) for s in places() if crosses(s, by)])


def send_far(x, by, dx, dy):
    return permute(x, [(moved(s, dx, dy), target(s, by)) for s in places() if crosses(s, by)])


def send_late(x, by):
    def inside(s):
        return (s[0],) + target(s, by)[1:]

    near = permute(x, [(s, inside(s)) for s in places()])
    return near, [(inside(s), target(s, by)) for s in places() if crosses(s, by)]


def from_far(by):
    inner = lax.axis_index("seq") % 16 - by
    return (inner < 0) | (inner >= 16)


def dot(a, b):
    return jnp.dot(a, b, preferred_element_type=F32)


def dot_nt(a, b):
    return lax.dot_general(a, b, (((1,), (1,)), ((), ())), preferred_element_type=F32)


def dot_tn(a, b):
    return lax.dot_general(a, b, (((0,), (0,)), ((), ())), preferred_element_type=F32)


def column(row):
    eye = lax.broadcasted_iota(jnp.int32, (ROWS, ROWS), 0) == lax.broadcasted_iota(jnp.int32, (ROWS, ROWS), 1)
    return jnp.sum(jnp.where(eye, row, 0.0), axis=1, keepdims=True)


def update(w, r, k, v, rates, store):
    ka = dot(k, r[0])
    kb = dot(k, r[1])
    s = jax.nn.sigmoid(ka)
    kas = ka * s
    kh = (kas * kb).astype(BF)
    sv = (rates * v.astype(F32)).astype(BF)
    bk = dot_nt(sv, r[2])
    d1 = (bk * kb * (s * (1.0 + ka * (1.0 - s)))).astype(BF)
    d3 = (bk * kas).astype(BF)
    for i, (a, b) in enumerate(((k, d1), (k, d3), (kh, sv))):
        for j in range(0, HD, 256):
            cols = slice(j, j + 256)
            old = w(i, cols)
            new = old + dot_tn(a, b[:, cols])
            before = jnp.mean(old * old, axis=0, keepdims=True) + EPS
            after = jnp.mean(new * new, axis=0, keepdims=True) + EPS
            store(i, cols, new * jnp.sqrt(before / after))


def fast_out(r, q, gain):
    qa = dot(q, r[0])
    qb = dot(q, r[1])
    qh = (qa * jax.nn.sigmoid(qa) * qb).astype(BF)
    fo = dot(qh, r[2])
    return fo * lax.rsqrt(jnp.mean(fo * fo, axis=1, keepdims=True) + EPS) * gain


def window(q, kp, k, vp, v):
    scale = HD**-0.5
    row = lax.broadcasted_iota(jnp.int32, (ROWS, ROWS), 0)
    col = lax.broadcasted_iota(jnp.int32, (ROWS, ROWS), 1)
    old = jnp.where(col > row, dot_nt(q, kp) * scale, -1e30)
    own = jnp.where(col <= row, dot_nt(q, k) * scale, -1e30)
    peak = jnp.maximum(jnp.max(old, axis=1, keepdims=True), jnp.max(own, axis=1, keepdims=True))
    old = jnp.exp(old - peak)
    own = jnp.exp(own - peak)
    total = jnp.sum(old, axis=1, keepdims=True) + jnp.sum(own, axis=1, keepdims=True)
    return dot((old / total).astype(BF), vp) + dot((own / total).astype(BF), v)


def project(cm, weight, give, own, far):
    head = lax.axis_index("head")
    z_lo, core = head // 2, head % 2

    def part(z, c):
        at = pl.multiple_of((z * 2 + c) * HD, HD)
        return dot(cm, weight[:, pl.ds(at, HD)]).astype(BF)

    give[1] = part(1 - z_lo, 1 - core)
    give[0] = part(z_lo, 1 - core)
    far[...] = part(1 - z_lo, core)
    own[...] = part(z_lo, core)


def pack_pair(keys, values, out, sems):
    copies = [pltpu.make_async_copy(a.at[2], out.at[i], sems.at[i]) for i, a in enumerate((keys, values))]
    for c in copies:
        c.start()
    for c in copies:
        c.wait()


def pack_rest(keys, values, queries, _, out, q1, sems):
    copies = [pltpu.make_async_copy(a.at[0], out.at[i], sems.at[i]) for i, a in enumerate((keys, values))]
    copies.append(pltpu.make_async_copy(queries.at[1], q1, sems.at[2]))
    for c in copies:
        c.start()
    for c in copies:
        c.wait()


def first_tick(u, k, v, rates, q, gain, state, normed):
    r = [u[0, 0, i].astype(BF) for i in range(3)]

    def store(i, cols, new):
        state[i, :, cols] = new

    update(lambda i, cols: u[0, 0, i, :, cols], r, k[0], v[0], column(rates[0]), store)
    normed[...] = fast_out(r, q[0], gain[...])


def second_tick(u, kv, rates, qn, qf, kp, vp, gain, one, rest, second, third, cm):
    r = [u[i].astype(BF) for i in range(3)]

    def store(i, cols, new):
        new = new.astype(BF)
        if i == 0:
            one[:, cols] = new
        else:
            rest[(i - 1) * HD : i * HD, cols] = new
            (second, third)[i - 1][:, cols] = new

    update(lambda i, cols: u[i, :, cols], r, kv[0], kv[1], column(rates[1]), store)
    q = jnp.where(from_far(-1), qf[...], qn[...])
    cm[...] = (window(q, kp[0], kv[0], vp[0], kv[1]) + fast_out(r, q, gain[...])).astype(BF)


def first_mix(q, kv, k, v, normed, cm):
    cm[...] = (window(q[0], kv[0], k[0], kv[1], v[0]) + normed[...]).astype(BF)


def project_two(cm0, cm1, weight, give, own, far):
    project(cm0[...], weight, give.at[0], own.at[0], far.at[0])
    project(cm1[...], weight, give.at[1], own.at[1], far.at[1])


def attend(q, kvn, kvf, k, v, att):
    late = from_far(1)
    kp = jnp.where(late, kvf[0], kvn[0])
    vp = jnp.where(late, kvf[1], kvn[1])
    att[...] = window(q[0], kp, k[0], vp, v[0])


def third_mix(a, near, bf, cf, q, att, gain, weight, give, own, far, m):
    late = from_far(2)
    m[:HD] = a[...]
    m[HD : 2 * HD] = jnp.where(late, bf[...], near[:HD])
    m[2 * HD :] = jnp.where(late, cf[...], near[HD:])
    r = [m[i * HD : (i + 1) * HD] for i in range(3)]
    cm = (att[...] + fast_out(r, q[0], gain[...])).astype(BF)
    project(cm, weight, give, own, far)


def third_update(m, k, v, rates, out):
    def store(i, cols, new):
        out[0, 0, i, :, cols] = new

    r = [m[i * HD : (i + 1) * HD] for i in range(3)]
    update(lambda i, cols: m[i * HD : (i + 1) * HD, cols].astype(F32), r, k[0], v[0], column(rates[2]), store)


def first_two(other, got, own, out):
    for t in range(2):
        out[t] = (got[t, 0].astype(F32) + own[t].astype(F32) + other[t].astype(F32)).astype(BF)


def last_one(_, other, got, own, out):
    out[0] = (got[0].astype(F32) + own[...].astype(F32) + other[...].astype(F32)).astype(BF)


LEAD = 40 * 10**9
WHOLE = pl.BlockSpec(memory_space=pltpu.VMEM)
HBM = pl.BlockSpec(memory_space=pl.ANY)


def slab(shape, index):
    return pl.BlockSpec(shape, lambda _, index=index: (index,) + (0,) * (len(shape) - 1))


def rows_of(t):
    return slab((1, ROWS, HD), t)


def call(body, outs, args, matmuls=0, scratch=(), lead=0, **more):
    return pl.pallas_call(
        body,
        out_shape=[jax.ShapeDtypeStruct(s, d) for s, d, _ in outs],
        grid=(1,),
        in_specs=[s for _, s in args],
        out_specs=[s for _, _, s in outs],
        scratch_shapes=list(scratch),
        compiler_params=pltpu.CompilerParams(vmem_limit_bytes=32 * 1024 * 1024),
        cost_estimate=pl.CostEstimate(flops=1024 * matmuls + lead, bytes_accessed=1024, transcendentals=0),
        **more,
    )(*[a for a, _ in args])


FLAT = ((ROWS, HD), BF, WHOLE)
WIDE = ((ROWS, HD), F32, WHOLE)
SUM = [((2, ROWS, HD), BF, WHOLE), FLAT, FLAT]
SUM_TWO = [((2, 2, ROWS, HD), BF, WHOLE), ((2, ROWS, HD), BF, WHOLE), ((2, ROWS, HD), BF, WHOLE)]
HALF = ((HD, HD), BF, WHOLE)
STATE = ((3, HD, HD), F32, WHOLE)


def head_sum(give, own, far):
    spots = places()
    got = permute(give, [(s, s[:3] + (s[3] ^ 1,)) for s in spots])
    pair = (got[..., 1, :, :].astype(F32) + far.astype(F32)).astype(BF)
    other = permute(pair, [(s, s[:3] + (s[3] ^ 2,)) for s in spots])
    return (other, WHOLE), (got, WHOLE), (own, WHOLE)


def after(x, *ys):
    return lax.optimization_barrier((x,) + ys)[0]


def on_device(queries, keys, values, rates, gain, weight, incoming):
    gain = gain.reshape(1, HD)
    rates = rates.reshape(3, 1, ROWS)
    rate = (rates, slab((3, 1, ROWS), 0))
    gain = (gain, slab((1, HD), 0))
    weight = (weight, slab((HD, 4 * HD), 0))

    (kv2,) = call(pack_pair, [((2, ROWS, HD), BF, HBM)], ((keys, HBM), (values, HBM)), scratch=[pltpu.SemaphoreType.DMA((2,))])
    kv0, q1 = call(
        pack_rest,
        [((2, ROWS, HD), BF, HBM), ((ROWS, HD), BF, HBM)],
        ((keys, HBM), (values, HBM), (queries, HBM), (kv2, HBM)),
        scratch=[pltpu.SemaphoreType.DMA((3,))],
    )
    next_rates = send_direct(rates, -1)
    next_kv = send_direct(kv2, -1)
    q1n, q1_pairs = send_late(q1, -1)
    kv2n, kv2_pairs = send_late(kv2, 1)
    q1f = permute(q1n, q1_pairs)
    kv2f = permute(kv2n, kv2_pairs)
    kv0 = send_direct(kv0, 1)

    state, normed0 = call(
        first_tick,
        [STATE, WIDE],
        (
            (after(incoming, next_rates, q1n), slab((1, 1, 3, HD, HD), 0)),
            (keys, rows_of(1)),
            (values, rows_of(1)),
            rate,
            (queries, rows_of(0)),
            gain,
        ),
        9,
        lead=LEAD,
    )
    a, bc, b, c, cm1 = call(
        second_tick,
        [HALF, ((2 * HD, HD), BF, WHOLE), HALF, HALF, FLAT],
        (
            (state, WHOLE),
            (next_kv, WHOLE),
            (next_rates, WHOLE),
            (q1n, WHOLE),
            (q1f, WHOLE),
            (keys, rows_of(1)),
            (values, rows_of(1)),
            gain,
        ),
        11,
        lead=LEAD,
    )
    c1 = send_first(c, 2, 0, -1)
    b1 = send_first(b, 2, 0, 1)
    a2, near = send_direct(a, 2), send_near(bc, 2)
    bf, cf = send_far(b1, 2, 0, 1), send_far(c1, 2, 0, -1)
    (cm0,) = call(
        first_mix,
        [FLAT],
        ((queries, rows_of(0)), (kv0, WHOLE), (keys, rows_of(1)), (values, rows_of(1)), (normed0, WHOLE)),
        2,
    )
    cm1 = send_direct(after(cm1, b1, c1), 1)
    (att2,) = call(
        attend, [WIDE], ((queries, rows_of(2)), (kv2n, WHOLE), (kv2f, WHOLE), (keys, rows_of(3)), (values, rows_of(3))), 2
    )
    two = head_sum(*call(project_two, SUM_TWO, ((after(cm0, att2), WHOLE), (cm1, WHOLE), weight), 8))
    (mixed,) = call(first_two, [((3, ROWS, HD), BF, slab((3, ROWS, HD), 0))], two)
    *sum2, m = call(
        third_mix,
        SUM + [((3 * HD, HD), BF, WHOLE)],
        (
            (a2, WHOLE),
            (near, WHOLE),
            (bf, WHOLE),
            (cf, WHOLE),
            (queries, rows_of(2)),
            (att2, WHOLE),
            gain,
            weight,
        ),
        7,
        lead=LEAD,
    )
    sum2 = head_sum(*sum2)
    (outgoing,) = call(
        third_update,
        [((1, 1, 3, HD, HD), F32, slab((1, 1, 3, HD, HD), 0))],
        ((m, WHOLE), (keys, rows_of(3)), (values, rows_of(3)), rate),
        6,
    )
    (mixed,) = call(
        last_one, [((3, ROWS, HD), BF, rows_of(2))], ((mixed, HBM),) + sum2, input_output_aliases={0: 0}
    )
    return mixed, outgoing


def solution(mesh):
    placed = (
        P(None, "seq", "head"),
        P(None, "seq", "head"),
        P(None, "seq", "head"),
        P(None, "seq", "head"),
        P("head"),
        P("head", None),
        P("seq", "head", None, None, None),
    )
    return jax.shard_map(
        on_device,
        mesh=mesh,
        in_specs=placed,
        out_specs=(P(None, "seq", "head"), P("seq", "head", None, None, None)),
        check_vma=False,
    )
```

```python
import functools

import jax
import jax.numpy as jnp
from jax import lax
from jax.experimental import pallas as pl
from jax.experimental.pallas import tpu as pltpu
from jax.sharding import PartitionSpec as P

BF = jnp.bfloat16
F32 = jnp.float32
ROWS, HD = 256, 512
EPS = 1e-06
NX, NY, NZH = 4, 4, 4
AXES = ("seq", "head")


def flat(spot):
    zh, y, x, head = spot
    return ((zh % NZH) * NY * NX + (y % NY) * NX + x % NX) * 4 + head


def places():
    return [(zh, y, x, h) for zh in range(NZH) for y in range(NY) for x in range(NX) for h in range(4)]


def target(spot, by):
    zh, y, x, head = spot
    block = (zh * 16 + y * 4 + x + by) % 64
    return (block // 16, block // 4 % 4, block % 4, head)


def crosses(spot, by):
    return target(spot, by)[0] != spot[0]


def moved(spot, dx, dy):
    zh, y, x, head = spot
    return (zh, (y + dy) % NY, (x + dx) % NX, head)


def permute(x, pairs):
    return lax.ppermute(x, AXES, [(flat(a), flat(b)) for a, b in pairs])


def send_direct(x, by):
    return permute(x, [(s, target(s, by)) for s in places()])


def send_near(x, by):
    return permute(x, [(s, target(s, by)) for s in places() if not crosses(s, by)])


def send_first(x, by, dx, dy):
    return permute(x, [(s, moved(s, dx, dy)) for s in places() if crosses(s, by)])


def send_far(x, by, dx, dy):
    return permute(x, [(moved(s, dx, dy), target(s, by)) for s in places() if crosses(s, by)])


def send_late(x, by):
    def inside(s):
        return (s[0],) + target(s, by)[1:]

    near = permute(x, [(s, inside(s)) for s in places()])
    return near, [(inside(s), target(s, by)) for s in places() if crosses(s, by)]


def from_far(by):
    inner = lax.axis_index("seq") % 16 - by
    return (inner < 0) | (inner >= 16)


def dot(a, b):
    return jnp.dot(a, b, preferred_element_type=F32)


def dot_nt(a, b):
    return lax.dot_general(a, b, (((1,), (1,)), ((), ())), preferred_element_type=F32)


def dot_tn(a, b):
    return lax.dot_general(a, b, (((0,), (0,)), ((), ())), preferred_element_type=F32)


def column(row):
    eye = lax.broadcasted_iota(jnp.int32, (ROWS, ROWS), 0) == lax.broadcasted_iota(jnp.int32, (ROWS, ROWS), 1)
    return jnp.sum(jnp.where(eye, row, 0.0), axis=1, keepdims=True)


def update(w, r, k, v, rates, store):
    ka = dot(k, r[0])
    kb = dot(k, r[1])
    s = jax.nn.sigmoid(ka)
    kas = ka * s
    kh = (kas * kb).astype(BF)
    sv = (rates * v.astype(F32)).astype(BF)
    bk = dot_nt(sv, r[2])
    d1 = (bk * kb * (s * (1.0 + ka * (1.0 - s)))).astype(BF)
    d3 = (bk * kas).astype(BF)
    for i, (a, b) in enumerate(((k, d1), (k, d3), (kh, sv))):
        for j in range(0, HD, 256):
            cols = slice(j, j + 256)
            old = w(i, cols)
            new = old + dot_tn(a, b[:, cols])
            before = jnp.mean(old * old, axis=0, keepdims=True) + EPS
            after = jnp.mean(new * new, axis=0, keepdims=True) + EPS
            store(i, cols, new * jnp.sqrt(before / after))


def fast_out(r, q, gain):
    qa = dot(q, r[0])
    qb = dot(q, r[1])
    qh = (qa * jax.nn.sigmoid(qa) * qb).astype(BF)
    fo = dot(qh, r[2])
    return fo * lax.rsqrt(jnp.mean(fo * fo, axis=1, keepdims=True) + EPS) * gain


def window(q, kp, k, vp, v):
    scale = HD**-0.5
    row = lax.broadcasted_iota(jnp.int32, (ROWS, ROWS), 0)
    col = lax.broadcasted_iota(jnp.int32, (ROWS, ROWS), 1)
    old = jnp.where(col > row, dot_nt(q, kp) * scale, -1e30)
    own = jnp.where(col <= row, dot_nt(q, k) * scale, -1e30)
    peak = jnp.maximum(jnp.max(old, axis=1, keepdims=True), jnp.max(own, axis=1, keepdims=True))
    old = jnp.exp(old - peak)
    own = jnp.exp(own - peak)
    total = jnp.sum(old, axis=1, keepdims=True) + jnp.sum(own, axis=1, keepdims=True)
    return dot((old / total).astype(BF), vp) + dot((own / total).astype(BF), v)


def project(cm, weight, give, own, far):
    head = lax.axis_index("head")
    z_lo, core = head // 2, head % 2

    def part(z, c):
        at = pl.multiple_of((z * 2 + c) * HD, HD)
        return dot(cm, weight[:, pl.ds(at, HD)]).astype(BF)

    give[1] = part(1 - z_lo, 1 - core)
    give[0] = part(z_lo, 1 - core)
    far[...] = part(1 - z_lo, core)
    own[...] = part(z_lo, core)


def pack_pair(keys, values, out, sems):
    copies = [pltpu.make_async_copy(a.at[2], out.at[i], sems.at[i]) for i, a in enumerate((keys, values))]
    for c in copies:
        c.start()
    for c in copies:
        c.wait()


def pack_rest(keys, values, queries, _, out, q1, sems):
    copies = [pltpu.make_async_copy(a.at[0], out.at[i], sems.at[i]) for i, a in enumerate((keys, values))]
    copies.append(pltpu.make_async_copy(queries.at[1], q1, sems.at[2]))
    for c in copies:
        c.start()
    for c in copies:
        c.wait()


def first_tick(u, k, v, rates, q, gain, state, normed):
    r = [u[0, 0, i].astype(BF) for i in range(3)]

    def store(i, cols, new):
        state[i, :, cols] = new

    update(lambda i, cols: u[0, 0, i, :, cols], r, k[0], v[0], column(rates[0]), store)
    normed[...] = fast_out(r, q[0], gain[...])


def second_tick(u, kv, rates, qn, qf, kp, vp, gain, one, rest, second, third, cm):
    r = [u[i].astype(BF) for i in range(3)]

    def store(i, cols, new):
        new = new.astype(BF)
        if i == 0:
            one[:, cols] = new
        else:
            rest[(i - 1) * HD : i * HD, cols] = new
            (second, third)[i - 1][:, cols] = new

    update(lambda i, cols: u[i, :, cols], r, kv[0], kv[1], column(rates[1]), store)
    q = jnp.where(from_far(-1), qf[...], qn[...])
    cm[...] = (window(q, kp[0], kv[0], vp[0], kv[1]) + fast_out(r, q, gain[...])).astype(BF)


def first_mix(q, kv, k, v, normed, cm):
    cm[...] = (window(q[0], kv[0], k[0], kv[1], v[0]) + normed[...]).astype(BF)


def project_two(cm0, cm1, weight, give, own, far):
    project(cm0[...], weight, give.at[0], own.at[0], far.at[0])
    project(cm1[...], weight, give.at[1], own.at[1], far.at[1])


def attend(q, kvn, kvf, k, v, att):
    late = from_far(1)
    kp = jnp.where(late, kvf[0], kvn[0])
    vp = jnp.where(late, kvf[1], kvn[1])
    att[...] = window(q[0], kp, k[0], vp, v[0])


def third_mix(a, near, bf, cf, q, att, gain, weight, give, own, far, m):
    late = from_far(2)
    m[:HD] = a[...]
    m[HD : 2 * HD] = jnp.where(late, bf[...], near[:HD])
    m[2 * HD :] = jnp.where(late, cf[...], near[HD:])
    r = [m[i * HD : (i + 1) * HD] for i in range(3)]
    cm = (att[...] + fast_out(r, q[0], gain[...])).astype(BF)
    project(cm, weight, give, own, far)


def third_update(m, k, v, rates, out):
    def store(i, cols, new):
        out[0, 0, i, :, cols] = new

    r = [m[i * HD : (i + 1) * HD] for i in range(3)]
    update(lambda i, cols: m[i * HD : (i + 1) * HD, cols].astype(F32), r, k[0], v[0], column(rates[2]), store)


def first_two(other, got, own, out):
    for t in range(2):
        out[t] = (got[t, 0].astype(F32) + own[t].astype(F32) + other[t].astype(F32)).astype(BF)


def last_one(_, other, got, own, out):
    out[0] = (got[0].astype(F32) + own[...].astype(F32) + other[...].astype(F32)).astype(BF)


LEAD = 40 * 10**9
WHOLE = pl.BlockSpec(memory_space=pltpu.VMEM)
HBM = pl.BlockSpec(memory_space=pl.ANY)


def slab(shape, index):
    return pl.BlockSpec(shape, lambda _, index=index: (index,) + (0,) * (len(shape) - 1))


def rows_of(t):
    return slab((1, ROWS, HD), t)


def call(body, outs, args, matmuls=0, scratch=(), lead=0, **more):
    return pl.pallas_call(
        body,
        out_shape=[jax.ShapeDtypeStruct(s, d) for s, d, _ in outs],
        grid=(1,),
        in_specs=[s for _, s in args],
        out_specs=[s for _, _, s in outs],
        scratch_shapes=list(scratch),
        compiler_params=pltpu.CompilerParams(vmem_limit_bytes=32 * 1024 * 1024),
        cost_estimate=pl.CostEstimate(flops=1024 * matmuls + lead, bytes_accessed=1024, transcendentals=0),
        **more,
    )(*[a for a, _ in args])


FLAT = ((ROWS, HD), BF, WHOLE)
WIDE = ((ROWS, HD), F32, WHOLE)
SUM = [((2, ROWS, HD), BF, WHOLE), FLAT, FLAT]
SUM_TWO = [((2, 2, ROWS, HD), BF, WHOLE), ((2, ROWS, HD), BF, WHOLE), ((2, ROWS, HD), BF, WHOLE)]
HALF = ((HD, HD), BF, WHOLE)
STATE = ((3, HD, HD), F32, WHOLE)


def head_sum(give, own, far):
    spots = places()
    got = permute(give, [(s, s[:3] + (s[3] ^ 1,)) for s in spots])
    pair = (got[..., 1, :, :].astype(F32) + far.astype(F32)).astype(BF)
    other = permute(pair, [(s, s[:3] + (s[3] ^ 2,)) for s in spots])
    return (other, WHOLE), (got, WHOLE), (own, WHOLE)


def after(x, *ys):
    return lax.optimization_barrier((x,) + ys)[0]


def on_device(queries, keys, values, rates, gain, weight, incoming):
    gain = gain.reshape(1, HD)
    rates = rates.reshape(3, 1, ROWS)
    rate = (rates, slab((3, 1, ROWS), 0))
    gain = (gain, slab((1, HD), 0))
    weight = (weight, slab((HD, 4 * HD), 0))

    (kv2,) = call(pack_pair, [((2, ROWS, HD), BF, HBM)], ((keys, HBM), (values, HBM)), scratch=[pltpu.SemaphoreType.DMA((2,))])
    kv0, q1 = call(
        pack_rest,
        [((2, ROWS, HD), BF, HBM), ((ROWS, HD), BF, HBM)],
        ((keys, HBM), (values, HBM), (queries, HBM), (kv2, HBM)),
        scratch=[pltpu.SemaphoreType.DMA((3,))],
    )
    next_rates = send_direct(rates, -1)
    next_kv = send_direct(kv2, -1)
    q1n, q1_pairs = send_late(q1, -1)
    kv2n, kv2_pairs = send_late(kv2, 1)
    q1f = permute(q1n, q1_pairs)
    kv2f = permute(kv2n, kv2_pairs)
    kv0 = send_direct(kv0, 1)

    state, normed0 = call(
        first_tick,
        [STATE, WIDE],
        (
            (after(incoming, next_rates, q1n), slab((1, 1, 3, HD, HD), 0)),
            (keys, rows_of(1)),
            (values, rows_of(1)),
            rate,
            (queries, rows_of(0)),
            gain,
        ),
        9,
        lead=LEAD,
    )
    a, bc, b, c, cm1 = call(
        second_tick,
        [HALF, ((2 * HD, HD), BF, WHOLE), HALF, HALF, FLAT],
        (
            (state, WHOLE),
            (next_kv, WHOLE),
            (next_rates, WHOLE),
            (q1n, WHOLE),
            (q1f, WHOLE),
            (keys, rows_of(1)),
            (values, rows_of(1)),
            gain,
        ),
        11,
        lead=LEAD,
    )
    c1 = send_first(c, 2, -1, -2)
    b1 = send_first(b, 2, 0, 1)
    a2, near = send_direct(a, 2), send_near(bc, 2)
    bf, cf = send_far(b1, 2, 0, 1), send_far(c1, 2, -1, -2)
    (cm0,) = call(
        first_mix,
        [FLAT],
        ((queries, rows_of(0)), (kv0, WHOLE), (keys, rows_of(1)), (values, rows_of(1)), (normed0, WHOLE)),
        2,
    )
    cm1 = send_direct(after(cm1, b1, c1), 1)
    (att2,) = call(
        attend, [WIDE], ((queries, rows_of(2)), (kv2n, WHOLE), (kv2f, WHOLE), (keys, rows_of(3)), (values, rows_of(3))), 2
    )
    two = head_sum(*call(project_two, SUM_TWO, ((after(cm0, att2), WHOLE), (cm1, WHOLE), weight), 8))
    (mixed,) = call(first_two, [((3, ROWS, HD), BF, slab((3, ROWS, HD), 0))], two)
    *sum2, m = call(
        third_mix,
        SUM + [((3 * HD, HD), BF, WHOLE)],
        (
            (a2, WHOLE),
            (near, WHOLE),
            (bf, WHOLE),
            (cf, WHOLE),
            (queries, rows_of(2)),
            (att2, WHOLE),
            gain,
            weight,
        ),
        7,
        lead=LEAD,
    )
    sum2 = head_sum(*sum2)
    (outgoing,) = call(
        third_update,
        [((1, 1, 3, HD, HD), F32, slab((1, 1, 3, HD, HD), 0))],
        ((m, WHOLE), (keys, rows_of(3)), (values, rows_of(3)), rate),
        6,
    )
    (mixed,) = call(
        last_one, [((3, ROWS, HD), BF, rows_of(2))], ((mixed, HBM),) + sum2, input_output_aliases={0: 0}
    )
    return mixed, outgoing


def solution(mesh):
    placed = (
        P(None, "seq", "head"),
        P(None, "seq", "head"),
        P(None, "seq", "head"),
        P(None, "seq", "head"),
        P("head"),
        P("head", None),
        P("seq", "head", None, None, None),
    )
    return jax.shard_map(
        on_device,
        mesh=mesh,
        in_specs=placed,
        out_specs=(P(None, "seq", "head"), P("seq", "head", None, None, None)),
        check_vma=False,
    )
```
